32 devices in a mesh: grp: 4 (over y, core), mem: 8 (over z, x).
Axes of the slice: x: 2, y: 2, z: 4, core: 2. Of those that a mesh axis runs over, the one named last changes fastest.
Arguments:
- v_stack: bfloat16 [32768, 512], P(('grp', 'mem')), may hold values from -0.1875 to 0.1875
- u_stack: bfloat16 [32768, 512], P(('grp', 'mem')), may hold values from -0.25 to 0.25
- warm_start: bfloat16 [32768, 256], P(('grp', 'mem')), may hold values from -3 to 3
- observed: bfloat16 [32768, 256], P(('grp', 'mem')), may hold values from -12 to 12, as said below
- owners: int32 [32, 4], replicated, may hold values from 0 to 31, as said below
- tile_ranks: int32 [32, 4], P(('grp', 'mem')), may hold values from 8 to 128
Outputs:
- model: float32 [32768, 256], P(('grp', 'mem'))
- residual: bfloat16 [32768, 256], P(('grp', 'mem'))
The draws below stay inside these ranges and needn't reach their ends.
Inputs may be any that keep to these rules, and one draw needn't show every extreme that they name: Writing d = g * 8 + m, owners[d, t] = ((g + a_t) mod 4) * 8 + (m + b_t) mod 8, where the offsets a_t differ over t, the offsets b_t differ over t, some slot has a_t = 3, some slot has a_t = 2, some slot has b_t = 7 and some slot has b_t = 4. `observed`: entries of one row block share a scale.
All inputs are finite; a program needn't handle non-finite values.
Results may differ from the reference program's by a relative error of at most 0.006.
Values may be sent and summed in bfloat16 or wider, within the bound.
A program may use at most 64 MiB of HBM per device.

```python
import jax
import jax.numpy as jnp
from jax import lax

BS = 1024
RMAX = 128
TPC = 4
RHS = 256
ITERS = 2
NORDER = 32768
N_GRP = 4
N_MEM = 8
DEVICES = 32


def offsets_with_top(key, count):
    first, second = jax.random.split(key, 2)
    half = count // 2
    rest = jax.random.permutation(first, count - 2).astype(jnp.int32)
    rest = jnp.where(rest < half, rest, rest + 1).astype(jnp.int32)
    chosen = jnp.concatenate([jnp.array([count - 1, half], dtype=jnp.int32), rest[:TPC - 2]])
    order = jax.random.permutation(second, TPC).astype(jnp.int32)
    return chosen[order].astype(jnp.int32)


def draw_owners(key, part):
    first, second = jax.random.split(jax.random.fold_in(key, 11), 2)
    leads = offsets_with_top(first, N_GRP)
    shifts = offsets_with_top(second, N_MEM)
    groups = jnp.arange(N_GRP, dtype=jnp.int32)[:, None]
    target_group = (groups + leads[None, :]) % N_GRP
    members = jnp.arange(N_MEM, dtype=jnp.int32)[:, None]
    target_member = (members + shifts[None, :]) % N_MEM
    owned = target_group[:, None, :] * N_MEM + target_member[None, :, :]
    return owned.reshape(N_GRP * N_MEM, TPC).astype(jnp.int32)


def draw_observed(key, part):
    first = jax.random.fold_in(jax.random.fold_in(key, 23), 0)
    rows = BS * DEVICES
    blocks = (jnp.arange(rows, dtype=jnp.int32) // BS).astype(jnp.float32)
    scales = 1.0 + 2.0 * blocks / max(DEVICES - 1, 1)
    values = jax.random.normal(first, (rows, RHS), jnp.float32) * scales[:, None]
    return jnp.clip(values, -12.0, 12.0).astype(jnp.bfloat16)


def with_ends(values, stream_key, least, high):
    spot = [jax.random.randint(jax.random.fold_in(stream_key, axis), (), 0, length) for axis, length in enumerate(values.shape)]
    longest = values.shape.index(max(values.shape))
    beside = spot[:longest] + [(spot[longest] + 1) % values.shape[longest]] + spot[longest + 1:]
    return values.at[tuple(spot)].set(least).at[tuple(beside)].set(high)


def block_levels(own_key, shape, shards, least, largest):
    factor_of, own = 1.0, jax.random.fold_in(own_key, 6)
    for dim, blocks in shards:
        draws = jnp.exp(jax.random.uniform(jax.random.fold_in(own, dim), (blocks,), jnp.float32, least / len(shards), largest / len(shards)))
        factor_of = factor_of * jnp.repeat(draws, shape[dim] // blocks).reshape([-1 if axis == dim else 1 for axis in range(len(shape))])
    return factor_of


def gaussian(rng, dims, spread, most, pieces=(), held_as=jnp.bfloat16):
    values = spread * jax.random.normal(rng, dims, jnp.float32)
    if pieces:
        values = values * block_levels(rng, dims, pieces, -0.22, 0.18)
    return jnp.clip(values, -most, most).astype(held_as)


def setup_inputs(seed: int = 0) -> dict:
    keys = jax.random.split(jax.random.key(seed), 7)
    v_stack = gaussian(keys[0], (NORDER, TPC * RMAX), BS ** -0.5, 0.1875, ((0, 32),))
    u_stack = gaussian(keys[1], (NORDER, TPC * RMAX), (TPC * RMAX) ** -0.5, 0.25, ((0, 32),))
    warm_start = gaussian(keys[2], (NORDER, RHS), 0.5, 3.0, ((0, 32),))
    observed = draw_observed(jax.random.fold_in(keys[6], 71), 0)
    owners = draw_owners(jax.random.fold_in(keys[6], 71), 0)
    tile_ranks = with_ends(jax.random.randint(keys[5], (DEVICES, TPC), RMAX // 16, RMAX + 1), jax.random.fold_in(keys[5], 1), RMAX // 16, RMAX).astype(jnp.int32)
    return {"v_stack": v_stack, "u_stack": u_stack, "warm_start": warm_start, "observed": observed, "owners": owners, "tile_ranks": tile_ranks}


def reference(v_stack, u_stack, warm_start, observed, owners, tile_ranks):
    right_bases = v_stack.reshape(DEVICES, BS, TPC * RMAX)
    left_bases = u_stack.reshape(DEVICES, BS, TPC * RMAX)
    live_rows = (jnp.arange(RMAX, dtype=jnp.int32)[None, None, :] < tile_ranks[:, :, None]).astype(jnp.float32)
    slot_ids = jnp.arange(TPC, dtype=jnp.int32)[None, :]
    column_ids = jnp.broadcast_to(jnp.arange(DEVICES, dtype=jnp.int32)[:, None], (DEVICES, TPC))
    sources = jnp.zeros((DEVICES, TPC), jnp.int32).at[owners, jnp.broadcast_to(slot_ids, (DEVICES, TPC))].set(column_ids)

    def right_product(pair):
        return jnp.dot(pair[0].T, pair[1], preferred_element_type=jnp.float32)

    def left_apply(pair):
        return jnp.dot(pair[0], pair[1].reshape(TPC * RMAX, RHS), preferred_element_type=jnp.float32)

    def forward(field):
        panels = lax.map(right_product, (right_bases, field)).reshape(DEVICES, TPC, RMAX, RHS)
        panels = (panels * live_rows[..., None]).astype(jnp.bfloat16)
        arrived = panels[sources, slot_ids]
        return lax.map(left_apply, (left_bases, arrived))

    def adjoint(field):
        panels = lax.map(right_product, (left_bases, field)).reshape(DEVICES, TPC, RMAX, RHS).astype(jnp.bfloat16)
        returned = panels[owners, slot_ids]
        masked = (returned * live_rows[..., None]).astype(jnp.bfloat16)
        return lax.map(left_apply, (right_bases, masked))

    start = warm_start.reshape(DEVICES, BS, RHS)
    model = start.astype(jnp.float32)
    residual = forward(start) - observed.reshape(DEVICES, BS, RHS).astype(jnp.float32)
    entries = float(NORDER * RHS)

    def iterate(index, carry):
        model, residual = carry
        huber_scale = 1.345 * jnp.sum(jnp.abs(residual)) / entries + 1e-6
        weights = huber_scale / jnp.maximum(jnp.abs(residual), huber_scale)
        weighted = (weights * residual).astype(jnp.bfloat16)
        gradient = adjoint(weighted)
        image_dir = forward(gradient.astype(jnp.bfloat16))
        step_size = jnp.sum(gradient * gradient) / (jnp.sum(weights * image_dir * image_dir) + 1e-6)
        return (model - step_size * gradient, residual - step_size * image_dir)

    model, residual = lax.fori_loop(0, ITERS, iterate, (model, residual))
    return model.reshape(NORDER, RHS), residual.reshape(NORDER, RHS).astype(jnp.bfloat16)
```

```python
import functools

import jax
import jax.numpy as jnp
from jax import lax
from jax.experimental import pallas as pl
from jax.experimental.pallas import tpu as pltpu
from jax.sharding import PartitionSpec as P

ITERS = 2
ROUTES = 1 + 2 * ITERS
SUMS = 2 * ITERS
CHUNK = 256
MESH = pl.DeviceIdType.MESH


def kernel(dims, offsets, tab_ref, rank_ref, v_ref, u_ref, x_ref, obs_ref, model_ref, out_ref,
           vt, ut, resid, weight, grad, image, field, zbuf, arrived, part, *rest):
    groups, members, slots, width, rows, cols = dims
    devices = groups * members
    count = len(offsets)
    gsend, rest = rest[:ROUTES], rest[ROUTES:]
    gbuf, rest = rest[:ROUTES], rest[ROUTES:]
    msend, rest = rest[:ROUTES], rest[ROUTES:]
    mbuf, rest = rest[:ROUTES], rest[ROUTES:]
    sums, rest = rest[:SUMS], rest[SUMS:]
    gs_sem, gr_sem, ms_sem, mr_sem, ss_sem, sr_sem = rest
    g = lax.axis_index("grp")
    m = lax.axis_index("mem")

    def peer(r):
        return (lax.rem(g + lax.div(r, members), groups), lax.rem(m + lax.rem(r, members), members))

    barrier = pltpu.get_barrier_semaphore()

    @pl.loop(1, devices)
    def _(r):
        pl.semaphore_signal(barrier, inc=1, device_id=peer(r), device_id_type=MESH)

    ranks = [rank_ref[0, t] for t in range(slots)]

    def total(values):
        return functools.reduce(lambda p, q: p + q, values)

    group_slot = [tab_ref[0, s] for s in range(groups)]
    member_src = [tab_ref[0, groups + k] for k in range(count)]
    place = [tab_ref[0, groups + count + t] for t in range(slots)]

    row_ids = lax.broadcasted_iota(jnp.int32, (width, cols), 0)
    live = [jnp.minimum(jnp.maximum(ranks[t] - row_ids, 0), 1).astype(jnp.float32) for t in range(slots)]
    pending = []

    def at(i):
        return pl.ds(i * CHUNK, CHUNK)

    chunks = rows // CHUNK

    def send(src, dst, send_sem, recv_sem, target):
        copy = pltpu.make_async_remote_copy(
            src_ref=src, dst_ref=dst, send_sem=send_sem, recv_sem=recv_sem,
            device_id=target, device_id_type=MESH)
        copy.start()
        pending.append(copy)
        return copy

    def route(i, back, meanwhile=None):
        copies = []
        for s in reversed(range(groups)):
            panel = zbuf[group_slot[s]]
            if s == 0:
                gbuf[i][0] = panel
            else:
                gsend[i][s] = panel
                step = groups - s if back else s
                copies.append(send(gsend[i].at[s], gbuf[i].at[s], gs_sem.at[i, s], gr_sem.at[i, s],
                                   (lax.rem(g + step, groups), m)))
        if meanwhile is not None:
            meanwhile()
        for copy in copies:
            copy.wait_recv()
        copies = []
        for k, o in enumerate(offsets):
            panel = gbuf[i][member_src[k]]
            if o == 0:
                mbuf[i][k] = panel
            else:
                msend[i][k] = panel
                step = members - o if back else o
                copies.append(send(msend[i].at[k], mbuf[i].at[k], ms_sem.at[i, k], mr_sem.at[i, k],
                                   (g, lax.rem(m + step, members))))
        for copy in copies:
            copy.wait_recv()
        for t in range(slots):
            panel = mbuf[i][place[t]]
            if back:
                panel = panel * live[t].astype(jnp.bfloat16)
            arrived[t * width:(t + 1) * width, :] = panel

    def fold(x):
        y = jnp.sum(x.reshape(x.shape[0] // 8, 8, cols), axis=0)
        return total(y[:, c:c + 128] for c in range(0, cols, 128))

    def all_sum(j, values):
        n = len(values)
        for q, value in enumerate(values):
            sums[j][0, q * 8:(q + 1) * 8] = value

        def put(r):
            return pltpu.make_async_remote_copy(
                src_ref=sums[j].at[0], dst_ref=sums[j].at[r], send_sem=ss_sem.at[j],
                recv_sem=sr_sem.at[j], device_id=peer(r), device_id_type=MESH)

        @pl.loop(1, devices)
        def _(r):
            put(r).start()

        rest_of = sums[j].at[pl.ds(1, devices - 1)]
        whole = pltpu.make_async_remote_copy(
            src_ref=rest_of, dst_ref=rest_of, send_sem=ss_sem.at[j],
            recv_sem=sr_sem.at[j], device_id=peer(1), device_id_type=MESH)
        whole.wait_recv()
        pending.append(whole)
        added = jnp.sum(sums[j][...], axis=0)
        return [jnp.sum(added[q * 8:(q + 1) * 8]) for q in range(n)]

    def project(basis_t, value_ref):
        return jnp.dot(basis_t[...], value_ref[...], preferred_element_type=jnp.float32)

    def project_forward(value_ref):
        z = project(vt, value_ref)
        for t in range(slots):
            panel = z[t * width:(t + 1) * width]
            zbuf[t] = (panel * live[t]).astype(jnp.bfloat16)

    def apply(basis, i):
        return jnp.dot(basis[at(i), :], arrived[...], preferred_element_type=jnp.float32)

    def transpose_u():
        ut[...] = u_ref[...].T

    vt[...] = v_ref[...].T
    project_forward(x_ref)
    pl.semaphore_wait(barrier, devices - 1)
    route(0, False, transpose_u)
    part_sum = jnp.zeros((8, 128), jnp.float32)
    for i in range(chunks):
        r = apply(u_ref, i) - obs_ref[at(i), :].astype(jnp.float32)
        resid[at(i), :] = r
        part_sum = part_sum + fold(jnp.abs(r))

    entries = float(rows * cols * devices)
    for it in range(ITERS):
        (spread,) = all_sum(2 * it, [part_sum])
        scale = 1.345 * spread / entries + 1e-06
        for i in range(chunks):
            r = resid[at(i), :]
            w = scale / jnp.maximum(jnp.abs(r), scale)
            weight[at(i), :] = w
            field[at(i), :] = (w * r).astype(jnp.bfloat16)
        z = project(ut, field).astype(jnp.bfloat16)
        for t in range(slots):
            zbuf[t] = z[t * width:(t + 1) * width]
        route(1 + 2 * it, True)
        grad_part = jnp.zeros((8, 128), jnp.float32)
        for i in range(chunks):
            d = apply(v_ref, i)
            grad[at(i), :] = d
            field[at(i), :] = d.astype(jnp.bfloat16)
        project_forward(field)

        def square():
            acc = jnp.zeros((8, 128), jnp.float32)
            for i in range(chunks):
                d = grad[at(i), :]
                acc = acc + fold(d * d)
            part[...] = acc

        route(2 + 2 * it, False, square)
        curve_part = jnp.zeros((8, 128), jnp.float32)
        for i in range(chunks):
            y = apply(u_ref, i)
            image[at(i), :] = y
            curve_part = curve_part + fold(weight[at(i), :] * y * y)
        grad_sum, curve_sum = all_sum(2 * it + 1, [part[...], curve_part])
        step = grad_sum / (curve_sum + 1e-06)
        part_sum = jnp.zeros((8, 128), jnp.float32)
        for i in range(chunks):
            r = resid[at(i), :] - step * image[at(i), :]
            if it < ITERS - 1:
                resid[at(i), :] = r
                part_sum = part_sum + fold(jnp.abs(r))
            else:
                out_ref[at(i), :] = r.astype(jnp.bfloat16)
            before = x_ref[at(i), :].astype(jnp.float32) if it == 0 else model_ref[at(i), :]
            model_ref[at(i), :] = before - step * grad[at(i), :]
    for copy in pending:
        copy.wait_send()


def on_device(groups, members, v_stack, u_stack, warm_start, observed, owners, tile_ranks):
    rows, stack = v_stack.shape
    cols = warm_start.shape[1]
    slots = owners.shape[1]
    width = stack // slots
    devices = groups * members
    offsets = tuple(range(members))
    dims = (groups, members, slots, width, rows, cols)
    f32, bf16 = jnp.float32, jnp.bfloat16
    vmem = pl.BlockSpec(memory_space=pltpu.VMEM)
    smem = pl.BlockSpec(memory_space=pltpu.SMEM)
    dma = pltpu.SemaphoreType.DMA
    count = len(offsets)
    scratch = [
        pltpu.VMEM((stack, rows), bf16), pltpu.VMEM((stack, rows), bf16),
        pltpu.VMEM((rows, cols), f32), pltpu.VMEM((rows, cols), f32),
        pltpu.VMEM((rows, cols), f32), pltpu.VMEM((rows, cols), f32),
        pltpu.VMEM((rows, cols), bf16), pltpu.VMEM((slots, width, cols), bf16),
        pltpu.VMEM((stack, cols), bf16), pltpu.VMEM((8, 128), f32),
    ]
    scratch += [pltpu.VMEM((groups, width, cols), bf16)] * (2 * ROUTES)
    scratch += [pltpu.VMEM((count, width, cols), bf16)] * (2 * ROUTES)
    scratch += [pltpu.VMEM((devices, 8 * (1 + j % 2), 128), f32) for j in range(SUMS)]
    scratch += [dma((ROUTES, groups)), dma((ROUTES, groups)), dma((ROUTES, count)), dma((ROUTES, count)),
                dma((SUMS,)), dma((SUMS,))]
    lead = owners[0] // members
    shift = owners[0] % members
    slot_ids = jnp.arange(slots, dtype=jnp.int32)
    member_hit = (shift[:, None] == jnp.array(offsets, jnp.int32)[None, :]).astype(jnp.int32)
    group_hit = (lead[:, None] == jnp.arange(groups, dtype=jnp.int32)[None, :]).astype(jnp.int32)
    table = jnp.concatenate([
        jnp.sum(group_hit * slot_ids[:, None], axis=0),
        jnp.sum(member_hit * lead[:, None], axis=0),
        jnp.sum(member_hit * jnp.arange(count, dtype=jnp.int32)[None, :], axis=1),
    ])[None, :]
    return pl.pallas_call(
        functools.partial(kernel, dims, offsets),
        out_shape=(jax.ShapeDtypeStruct((rows, cols), f32), jax.ShapeDtypeStruct((rows, cols), bf16)),
        in_specs=[smem, smem, vmem, vmem, vmem, vmem],
        out_specs=(vmem, vmem),
        scratch_shapes=scratch,
        compiler_params=pltpu.CompilerParams(
            collective_id=0, has_side_effects=True, vmem_limit_bytes=60 * 1024 * 1024),
        cost_estimate=pl.CostEstimate(flops=10 * 2 * rows * stack * cols, bytes_accessed=8 * rows * stack, transcendentals=0),
    )(table, tile_ranks, v_stack, u_stack, warm_start, observed)


def solution(mesh):
    split = P(("grp", "mem"), None)
    return jax.shard_map(
        functools.partial(on_device, mesh.shape["grp"], mesh.shape["mem"]),
        mesh=mesh,
        in_specs=(split, split, split, split, P(), split),
        out_specs=(split, split),
        check_vma=False,
    )
```

```python
import functools

import jax
import jax.numpy as jnp
from jax import lax
from jax.experimental import pallas as pl
from jax.experimental.pallas import tpu as pltpu
from jax.sharding import PartitionSpec as P

ITERS = 2
ROUTES = 1 + 2 * ITERS
SUMS = 2 * ITERS
CHUNK = 256
HALVES = 1
PARTS = ROUTES * HALVES
MESH = pl.DeviceIdType.MESH


def kernel(dims, offsets, tab_ref, rank_ref, v_ref, u_ref, x_ref, obs_ref, model_ref, out_ref,
           vt, ut, resid, weight, grad, image, field, zbuf, arrived, part, *rest):
    groups, members, slots, width, rows, cols = dims
    devices = groups * members
    count = len(offsets)
    gsend, rest = rest[:PARTS], rest[PARTS:]
    gbuf, rest = rest[:PARTS], rest[PARTS:]
    msend, rest = rest[:PARTS], rest[PARTS:]
    mbuf, rest = rest[:PARTS], rest[PARTS:]
    sums, rest = rest[:SUMS], rest[SUMS:]
    gs_sem, gr_sem, ms_sem, mr_sem, ss_sem, sr_sem = rest
    g = lax.axis_index("grp")
    m = lax.axis_index("mem")

    def peer(r):
        if isinstance(r, int):
            return (lax.rem(g + r // members, groups), lax.rem(m + r % members, members))
        return (lax.rem(g + lax.div(r, members), groups), lax.rem(m + lax.rem(r, members), members))

    barrier = pltpu.get_barrier_semaphore()

    @pl.loop(1, devices)
    def _(r):
        pl.semaphore_signal(barrier, inc=1, device_id=peer(r), device_id_type=MESH)

    ranks = [rank_ref[0, t] for t in range(slots)]

    def total(values):
        return functools.reduce(lambda p, q: p + q, values)

    group_slot = [tab_ref[0, s] for s in range(groups)]
    member_src = [tab_ref[0, groups + k] for k in range(count)]
    place = [tab_ref[0, groups + count + t] for t in range(slots)]

    row_ids = lax.broadcasted_iota(jnp.int32, (width, cols), 0)
    live = [jnp.minimum(jnp.maximum(ranks[t] - row_ids, 0), 1).astype(jnp.float32) for t in range(slots)]
    pending = []

    def at(i):
        return pl.ds(i * CHUNK, CHUNK)

    chunks = rows // CHUNK

    def lanes(h):
        return slice(h * (cols // HALVES), (h + 1) * (cols // HALVES))

    def send(src, dst, send_sem, recv_sem, target):
        copy = pltpu.make_async_remote_copy(
            src_ref=src, dst_ref=dst, send_sem=send_sem, recv_sem=recv_sem,
            device_id=target, device_id_type=MESH)
        copy.start()
        pending.append(copy)
        return copy

    def route(i, back, meanwhile=None):
        sent = []
        for h in range(HALVES):
            q = i * HALVES + h
            copies = []
            for s in reversed(range(groups)):
                panel = zbuf[group_slot[s], :, lanes(h)]
                if s == 0:
                    gbuf[q][0] = panel
                else:
                    gsend[q][s] = panel
                    step = groups - s if back else s
                    copies.append(send(gsend[q].at[s], gbuf[q].at[s], gs_sem.at[q, s], gr_sem.at[q, s],
                                       (lax.rem(g + step, groups), m)))
            sent.append(copies)
        if meanwhile is not None:
            meanwhile()
        moved = []
        for h in range(HALVES):
            q = i * HALVES + h
            for copy in sent[h]:
                copy.wait_recv()
            copies = []
            for k, o in enumerate(offsets):
                panel = gbuf[q][member_src[k]]
                if o == 0:
                    mbuf[q][k] = panel
                else:
                    msend[q][k] = panel
                    step = members - o if back else o
                    copies.append(send(msend[q].at[k], mbuf[q].at[k], ms_sem.at[q, k], mr_sem.at[q, k],
                                       (g, lax.rem(m + step, members))))
            moved.append(copies)
        for h in range(HALVES):
            q = i * HALVES + h
            for copy in moved[h]:
                copy.wait_recv()
            for t in range(slots):
                panel = mbuf[q][place[t]]
                if back:
                    panel = panel * live[t][:, lanes(h)].astype(jnp.bfloat16)
                arrived[t * width:(t + 1) * width, lanes(h)] = panel

    def fold(x):
        y = jnp.sum(x.reshape(x.shape[0] // 8, 8, cols), axis=0)
        return total(y[:, c:c + 128] for c in range(0, cols, 128))

    def all_sum(j, values):
        n = len(values)
        for q, value in enumerate(values):
            sums[j][0, q:q + 1] = jnp.sum(value, axis=0, keepdims=True)

        def put(r):
            return pltpu.make_async_remote_copy(
                src_ref=sums[j].at[0], dst_ref=sums[j].at[r], send_sem=ss_sem.at[j],
                recv_sem=sr_sem.at[j], device_id=peer(r), device_id_type=MESH)

        for r in range(1, min(devices, 64)):
            put(r).start()

        if devices > 64:
            @pl.loop(64, devices)
            def _(r):
                put(r).start()

        rest_of = sums[j].at[pl.ds(1, devices - 1)]
        whole = pltpu.make_async_remote_copy(
            src_ref=rest_of, dst_ref=rest_of, send_sem=ss_sem.at[j],
            recv_sem=sr_sem.at[j], device_id=peer(1), device_id_type=MESH)
        whole.wait_recv()
        pending.append(whole)
        added = jnp.sum(sums[j][...], axis=0)
        return [jnp.sum(added[q:q + 1]) for q in range(n)]

    def project(basis_t, value_ref):
        return jnp.dot(basis_t[...], value_ref[...], preferred_element_type=jnp.float32)

    def project_forward(value_ref):
        z = project(vt, value_ref)
        for t in range(slots):
            panel = z[t * width:(t + 1) * width]
            zbuf[t] = (panel * live[t]).astype(jnp.bfloat16)

    def apply(basis, i):
        return jnp.dot(basis[at(i), :], arrived[...], preferred_element_type=jnp.float32)

    def transpose_u():
        ut[...] = u_ref[...].T

    vt[...] = v_ref[...].T
    project_forward(x_ref)
    pl.semaphore_wait(barrier, devices - 1)
    route(0, False, transpose_u)
    part_sum = jnp.zeros((8, 128), jnp.float32)
    for i in range(chunks):
        r = apply(u_ref, i) - obs_ref[at(i), :].astype(jnp.float32)
        resid[at(i), :] = r
        part_sum = part_sum + fold(jnp.abs(r))

    entries = float(rows * cols * devices)
    for it in range(ITERS):
        (spread,) = all_sum(2 * it, [part_sum])
        scale = 1.345 * spread / entries + 1e-06
        for i in range(chunks):
            r = resid[at(i), :]
            w = scale / jnp.maximum(jnp.abs(r), scale)
            weight[at(i), :] = w
            field[at(i), :] = (w * r).astype(jnp.bfloat16)
        z = project(ut, field).astype(jnp.bfloat16)
        for t in range(slots):
            zbuf[t] = z[t * width:(t + 1) * width]
        route(1 + 2 * it, True)
        grad_part = jnp.zeros((8, 128), jnp.float32)
        for i in range(chunks):
            d = apply(v_ref, i)
            grad[at(i), :] = d
            field[at(i), :] = d.astype(jnp.bfloat16)
        project_forward(field)

        def square():
            acc = jnp.zeros((8, 128), jnp.float32)
            for i in range(chunks):
                d = grad[at(i), :]
                acc = acc + fold(d * d)
            part[...] = acc

        route(2 + 2 * it, False, square)
        curve_part = jnp.zeros((8, 128), jnp.float32)
        for i in range(chunks):
            y = apply(u_ref, i)
            image[at(i), :] = y
            curve_part = curve_part + fold(weight[at(i), :] * y * y)
        grad_sum, curve_sum = all_sum(2 * it + 1, [part[...], curve_part])
        step = grad_sum / (curve_sum + 1e-06)
        part_sum = jnp.zeros((8, 128), jnp.float32)
        for i in range(chunks):
            r = resid[at(i), :] - step * image[at(i), :]
            if it < ITERS - 1:
                resid[at(i), :] = r
                part_sum = part_sum + fold(jnp.abs(r))
            else:
                out_ref[at(i), :] = r.astype(jnp.bfloat16)
            before = x_ref[at(i), :].astype(jnp.float32) if it == 0 else model_ref[at(i), :]
            model_ref[at(i), :] = before - step * grad[at(i), :]
    for copy in pending:
        copy.wait_send()


def on_device(groups, members, v_stack, u_stack, warm_start, observed, owners, tile_ranks):
    rows, stack = v_stack.shape
    cols = warm_start.shape[1]
    slots = owners.shape[1]
    width = stack // slots
    devices = groups * members
    offsets = tuple(sorted(range(members), key=lambda o: -min(o, members - o)))
    dims = (groups, members, slots, width, rows, cols)
    f32, bf16 = jnp.float32, jnp.bfloat16
    vmem = pl.BlockSpec(memory_space=pltpu.VMEM)
    smem = pl.BlockSpec(memory_space=pltpu.SMEM)
    dma = pltpu.SemaphoreType.DMA
    count = len(offsets)
    scratch = [
        pltpu.VMEM((stack, rows), bf16), pltpu.VMEM((stack, rows), bf16),
        pltpu.VMEM((rows, cols), f32), pltpu.VMEM((rows, cols), f32),
        pltpu.VMEM((rows, cols), f32), pltpu.VMEM((rows, cols), f32),
        pltpu.VMEM((rows, cols), bf16), pltpu.VMEM((slots, width, cols), bf16),
        pltpu.VMEM((stack, cols), bf16), pltpu.VMEM((8, 128), f32),
    ]
    scratch += [pltpu.VMEM((groups, width, cols // HALVES), bf16)] * (2 * PARTS)
    scratch += [pltpu.VMEM((count, width, cols // HALVES), bf16)] * (2 * PARTS)
    scratch += [pltpu.VMEM((devices, 1 + j % 2, 128), f32) for j in range(SUMS)]
    scratch += [dma((PARTS, groups)), dma((PARTS, groups)), dma((PARTS, count)), dma((PARTS, count)),
                dma((SUMS,)), dma((SUMS,))]
    lead = owners[0] // members
    shift = owners[0] % members
    slot_ids = jnp.arange(slots, dtype=jnp.int32)
    member_hit = (shift[:, None] == jnp.array(offsets, jnp.int32)[None, :]).astype(jnp.int32)
    group_hit = (lead[:, None] == jnp.arange(groups, dtype=jnp.int32)[None, :]).astype(jnp.int32)
    table = jnp.concatenate([
        jnp.sum(group_hit * slot_ids[:, None], axis=0),
        jnp.sum(member_hit * lead[:, None], axis=0),
        jnp.sum(member_hit * jnp.arange(count, dtype=jnp.int32)[None, :], axis=1),
    ])[None, :]
    return pl.pallas_call(
        functools.partial(kernel, dims, offsets),
        out_shape=(jax.ShapeDtypeStruct((rows, cols), f32), jax.ShapeDtypeStruct((rows, cols), bf16)),
        in_specs=[smem, smem, vmem, vmem, vmem, vmem],
        out_specs=(vmem, vmem),
        scratch_shapes=scratch,
        compiler_params=pltpu.CompilerParams(
            collective_id=0, has_side_effects=True, vmem_limit_bytes=60 * 1024 * 1024),
        cost_estimate=pl.CostEstimate(flops=10 * 2 * rows * stack * cols, bytes_accessed=8 * rows * stack, transcendentals=0),
    )(table, tile_ranks, v_stack, u_stack, warm_start, observed)


def solution(mesh):
    split = P(("grp", "mem"), None)
    return jax.shard_map(
        functools.partial(on_device, mesh.shape["grp"], mesh.shape["mem"]),
        mesh=mesh,
        in_specs=(split, split, split, split, P(), split),
        out_specs=(split, split),
        check_vma=False,
    )
```

```python
import functools

import jax
import jax.numpy as jnp
from jax import lax
from jax.experimental import pallas as pl
from jax.experimental.pallas import tpu as pltpu
from jax.sharding import PartitionSpec as P

ITERS = 2
ROUTES = 1 + 2 * ITERS
SUMS = 2 * ITERS
CHUNK = 256
HALVES = 1
PARTS = ROUTES * HALVES
MESH = pl.DeviceIdType.MESH


def kernel(dims, offsets, tab_ref, rank_ref, v_ref, u_ref, x_ref, obs_ref, model_ref, out_ref,
           vt, ut, resid, weight, grad, image, field, zbuf, arrived, part, *rest):
    groups, members, slots, width, rows, cols = dims
    devices = groups * members
    count = len(offsets)
    gsend, rest = rest[:PARTS], rest[PARTS:]
    gbuf, rest = rest[:PARTS], rest[PARTS:]
    msend, rest = rest[:PARTS], rest[PARTS:]
    mbuf, rest = rest[:PARTS], rest[PARTS:]
    sums, rest = rest[:SUMS], rest[SUMS:]
    gs_sem, gr_sem, ms_sem, mr_sem, ss_sem, sr_sem = rest
    g = lax.axis_index("grp")
    m = lax.axis_index("mem")

    def peer(r):
        if isinstance(r, int):
            return (lax.rem(g + r // members, groups), lax.rem(m + r % members, members))
        return (lax.rem(g + lax.div(r, members), groups), lax.rem(m + lax.rem(r, members), members))

    barrier = pltpu.get_barrier_semaphore()

    @pl.loop(1, devices)
    def _(r):
        pl.semaphore_signal(barrier, inc=1, device_id=peer(r), device_id_type=MESH)

    ranks = [rank_ref[0, t] for t in range(slots)]

    def total(values):
        return functools.reduce(lambda p, q: p + q, values)

    group_slot = [tab_ref[0, s] for s in range(groups)]
    member_src = [tab_ref[0, groups + k] for k in range(count)]
    place = [tab_ref[0, groups + count + t] for t in range(slots)]

    row_ids = lax.broadcasted_iota(jnp.int32, (width, cols), 0)
    live = [jnp.minimum(jnp.maximum(ranks[t] - row_ids, 0), 1).astype(jnp.float32) for t in range(slots)]
    pending = []

    def at(i):
        return pl.ds(i * CHUNK, CHUNK)

    chunks = rows // CHUNK

    def lanes(h):
        return slice(h * (cols // HALVES), (h + 1) * (cols // HALVES))

    def send(src, dst, send_sem, recv_sem, target):
        copy = pltpu.make_async_remote_copy(
            src_ref=src, dst_ref=dst, send_sem=send_sem, recv_sem=recv_sem,
            device_id=target, device_id_type=MESH)
        copy.start()
        pending.append(copy)
        return copy

    def route(i, back, meanwhile=None):
        sent = []
        for h in range(HALVES):
            q = i * HALVES + h
            copies = []
            for s in reversed(range(groups)):
                panel = zbuf[group_slot[s], :, lanes(h)]
                if s == 0:
                    gbuf[q][0] = panel
                else:
                    gsend[q][s] = panel
                    step = groups - s if back else s
                    copies.append(send(gsend[q].at[s], gbuf[q].at[s], gs_sem.at[q, s], gr_sem.at[q, s],
                                       (lax.rem(g + step, groups), m)))
            sent.append(copies)
        if meanwhile is not None:
            meanwhile()
        moved = []
        for h in range(HALVES):
            q = i * HALVES + h
            for copy in sent[h]:
                copy.wait_recv()
            copies = []
            for k, o in enumerate(offsets):
                panel = gbuf[q][member_src[k]]
                if o == 0:
                    mbuf[q][k] = panel
                else:
                    msend[q][k] = panel
                    step = members - o if back else o
                    copies.append(send(msend[q].at[k], mbuf[q].at[k], ms_sem.at[q, k], mr_sem.at[q, k],
                                       (g, lax.rem(m + step, members))))
            moved.append(copies)
        for h in range(HALVES):
            q = i * HALVES + h
            for copy in moved[h]:
                copy.wait_recv()
            for t in range(slots):
                panel = mbuf[q][place[t]]
                if back:
                    panel = panel * live[t][:, lanes(h)].astype(jnp.bfloat16)
                arrived[t * width:(t + 1) * width, lanes(h)] = panel

    def fold(x):
        y = jnp.sum(x.reshape(x.shape[0] // 8, 8, cols), axis=0)
        return total(y[:, c:c + 128] for c in range(0, cols, 128))

    def all_sum(j, values, meanwhile=None):
        n = len(values)
        for q, value in enumerate(values):
            sums[j][0, q:q + 1] = jnp.sum(value, axis=0, keepdims=True)

        def put(r):
            return pltpu.make_async_remote_copy(
                src_ref=sums[j].at[0], dst_ref=sums[j].at[r], send_sem=ss_sem.at[j],
                recv_sem=sr_sem.at[j], device_id=peer(r), device_id_type=MESH)

        for r in range(1, min(devices, 64)):
            put(r).start()

        if devices > 64:
            @pl.loop(64, devices)
            def _(r):
                put(r).start()

        if meanwhile is not None:
            meanwhile()
        rest_of = sums[j].at[pl.ds(1, devices - 1)]
        whole = pltpu.make_async_remote_copy(
            src_ref=rest_of, dst_ref=rest_of, send_sem=ss_sem.at[j],
            recv_sem=sr_sem.at[j], device_id=peer(1), device_id_type=MESH)
        whole.wait_recv()
        pending.append(whole)
        added = jnp.sum(sums[j][...], axis=0)
        return [jnp.sum(added[q:q + 1]) for q in range(n)]

    def project(basis_t, value_ref):
        return jnp.dot(basis_t[...], value_ref[...], preferred_element_type=jnp.float32)

    def project_forward(value_ref):
        z = project(vt, value_ref)
        for t in range(slots):
            panel = z[t * width:(t + 1) * width]
            zbuf[t] = (panel * live[t]).astype(jnp.bfloat16)

    def apply(basis, i):
        return jnp.dot(basis[at(i), :], arrived[...], preferred_element_type=jnp.float32)

    def transpose_u():
        ut[...] = u_ref[...].T

    vt[...] = v_ref[...].T
    project_forward(x_ref)
    pl.semaphore_wait(barrier, devices - 1)
    route(0, False, transpose_u)
    part_sum = jnp.zeros((8, 128), jnp.float32)
    for i in range(chunks):
        r = apply(u_ref, i) - obs_ref[at(i), :].astype(jnp.float32)
        resid[at(i), :] = r
        part_sum = part_sum + fold(jnp.abs(r))

    entries = float(rows * cols * devices)
    late = None
    for it in range(ITERS):
        (spread,) = all_sum(2 * it, [part_sum], late)
        scale = 1.345 * spread / entries + 1e-06
        for i in range(chunks):
            r = resid[at(i), :]
            w = scale / jnp.maximum(jnp.abs(r), scale)
            weight[at(i), :] = w
            field[at(i), :] = (w * r).astype(jnp.bfloat16)
        z = project(ut, field).astype(jnp.bfloat16)
        for t in range(slots):
            zbuf[t] = z[t * width:(t + 1) * width]
        route(1 + 2 * it, True)
        grad_part = jnp.zeros((8, 128), jnp.float32)
        for i in range(chunks):
            d = apply(v_ref, i)
            grad[at(i), :] = d
            field[at(i), :] = d.astype(jnp.bfloat16)
        project_forward(field)

        def square():
            acc = jnp.zeros((8, 128), jnp.float32)
            for i in range(chunks):
                d = grad[at(i), :]
                acc = acc + fold(d * d)
            part[...] = acc

        route(2 + 2 * it, False, square)
        curve_part = jnp.zeros((8, 128), jnp.float32)
        for i in range(chunks):
            y = apply(u_ref, i)
            image[at(i), :] = y
            curve_part = curve_part + fold(weight[at(i), :] * y * y)
        grad_sum, curve_sum = all_sum(2 * it + 1, [part[...], curve_part])
        step = grad_sum / (curve_sum + 1e-06)
        part_sum = jnp.zeros((8, 128), jnp.float32)
        for i in range(chunks):
            r = resid[at(i), :] - step * image[at(i), :]
            if it < ITERS - 1:
                resid[at(i), :] = r
                part_sum = part_sum + fold(jnp.abs(r))
            else:
                out_ref[at(i), :] = r.astype(jnp.bfloat16)

        def late(first=it == 0, step=step):
            for i in range(chunks):
                before = x_ref[at(i), :].astype(jnp.float32) if first else model_ref[at(i), :]
                model_ref[at(i), :] = before - step * grad[at(i), :]

    late()
    for copy in pending:
        copy.wait_send()


def on_device(groups, members, v_stack, u_stack, warm_start, observed, owners, tile_ranks):
    rows, stack = v_stack.shape
    cols = warm_start.shape[1]
    slots = owners.shape[1]
    width = stack // slots
    devices = groups * members
    offsets = tuple(sorted(range(members), key=lambda o: -min(o, members - o)))
    dims = (groups, members, slots, width, rows, cols)
    f32, bf16 = jnp.float32, jnp.bfloat16
    vmem = pl.BlockSpec(memory_space=pltpu.VMEM)
    smem = pl.BlockSpec(memory_space=pltpu.SMEM)
    dma = pltpu.SemaphoreType.DMA
    count = len(offsets)
    scratch = [
        pltpu.VMEM((stack, rows), bf16), pltpu.VMEM((stack, rows), bf16),
        pltpu.VMEM((rows, cols), f32), pltpu.VMEM((rows, cols), f32),
        pltpu.VMEM((rows, cols), f32), pltpu.VMEM((rows, cols), f32),
        pltpu.VMEM((rows, cols), bf16), pltpu.VMEM((slots, width, cols), bf16),
        pltpu.VMEM((stack, cols), bf16), pltpu.VMEM((8, 128), f32),
    ]
    scratch += [pltpu.VMEM((groups, width, cols // HALVES), bf16)] * (2 * PARTS)
    scratch += [pltpu.VMEM((count, width, cols // HALVES), bf16)] * (2 * PARTS)
    scratch += [pltpu.VMEM((devices, 1 + j % 2, 128), f32) for j in range(SUMS)]
    scratch += [dma((PARTS, groups)), dma((PARTS, groups)), dma((PARTS, count)), dma((PARTS, count)),
                dma((SUMS,)), dma((SUMS,))]
    lead = owners[0] // members
    shift = owners[0] % members
    slot_ids = jnp.arange(slots, dtype=jnp.int32)
    member_hit = (shift[:, None] == jnp.array(offsets, jnp.int32)[None, :]).astype(jnp.int32)
    group_hit = (lead[:, None] == jnp.arange(groups, dtype=jnp.int32)[None, :]).astype(jnp.int32)
    table = jnp.concatenate([
        jnp.sum(group_hit * slot_ids[:, None], axis=0),
        jnp.sum(member_hit * lead[:, None], axis=0),
        jnp.sum(member_hit * jnp.arange(count, dtype=jnp.int32)[None, :], axis=1),
    ])[None, :]
    return pl.pallas_call(
        functools.partial(kernel, dims, offsets),
        out_shape=(jax.ShapeDtypeStruct((rows, cols), f32), jax.ShapeDtypeStruct((rows, cols), bf16)),
        in_specs=[smem, smem, vmem, vmem, vmem, vmem],
        out_specs=(vmem, vmem),
        scratch_shapes=scratch,
        compiler_params=pltpu.CompilerParams(
            collective_id=0, has_side_effects=True, vmem_limit_bytes=60 * 1024 * 1024),
        cost_estimate=pl.CostEstimate(flops=10 * 2 * rows * stack * cols, bytes_accessed=8 * rows * stack, transcendentals=0),
    )(table, tile_ranks, v_stack, u_stack, warm_start, observed)


def solution(mesh):
    split = P(("grp", "mem"), None)
    return jax.shard_map(
        functools.partial(on_device, mesh.shape["grp"], mesh.shape["mem"]),
        mesh=mesh,
        in_specs=(split, split, split, split, P(), split),
        out_specs=(split, split),
        check_vma=False,
    )
```
